512 devices in a mesh: gx: 32 (over z, x_lo, core), gy: 16 (over y, x_hi).
Axes of the slice: x: 4 (x_hi: 2, x_lo: 2; x = x_hi * 2 + x_lo), y: 8, z: 8, core: 2. Of those that a mesh axis runs over, the one named last changes fastest.
Arguments:
- green: bfloat16 [32, 16, 1024, 1024], P('gx', 'gy'), may hold values from -0.1875 to 0.1875
- sources: bfloat16 [6, 32, 16, 768, 128], P(None, 'gx', 'gy'), may hold values from -3 to 3
- entering: float32 [32, 16, 1024, 128], P('gx', 'gy'), may hold values from -6 to 6
- start_front: int32 [24], replicated, may hold values from -5 to 41, as said below
Outputs:
- last_traces: float32 [32, 16, 1024, 128], P('gx', 'gy')
The draws below stay inside these ranges and needn't reach their ends.
Inputs may be any that keep to these rules, and one draw needn't show every extreme that they name: `start_front`: the 24 values are distinct.
All inputs are finite; a program needn't handle non-finite values.
Results may differ from the reference program's by a relative error of at most 0.0055.
Values may be sent and summed in bfloat16 or wider, within the bound.
A program may use at most 64 MiB of HBM per device.

```python
import jax
import jax.numpy as jnp
from jax import lax

TRACE = 384
BS = 128
TICKS = 6
ORDER = 1024
FRONTS = 47
NB = 24
N_GX = 32
N_GY = 16


def draw_start_front(key, part):
    shuffled = jax.random.permutation(key, FRONTS)
    return (shuffled[:NB] + (1 - TICKS)).astype(jnp.int32)


def shard_levels(stream_key, shape, cuts, low, top_value):
    loudness, own = 1.0, jax.random.fold_in(stream_key, 6)
    for position, parts in cuts:
        draws = jnp.exp(jax.random.uniform(jax.random.fold_in(own, position), (parts,), jnp.float32, low / len(cuts), top_value / len(cuts)))
        loudness = loudness * jnp.repeat(draws, shape[position] // parts).reshape([-1 if axis == position else 1 for axis in range(len(shape))])
    return loudness


def normal_values(stream_key, extent, scale, reach, cuts=(), kind=jnp.bfloat16):
    gain = shard_levels(stream_key, extent, cuts, -0.22, 0.18) if cuts else 1.0
    result = jax.random.normal(stream_key, extent, jnp.float32) * scale * gain
    return jnp.minimum(jnp.maximum(result, -reach), reach).astype(kind)


def setup_inputs(seed: int = 0) -> dict:
    arg_keys = jax.random.split(jax.random.key(seed), 5)
    green = normal_values(arg_keys[0], (N_GX, N_GY, ORDER, ORDER), ORDER ** -0.5, 0.1875, ((0, 32), (1, 16)))
    sources = normal_values(arg_keys[1], (TICKS, N_GX, N_GY, 2 * TRACE, BS), 0.5, 3.0, ((1, 32), (2, 16)))
    entering = normal_values(arg_keys[2], (N_GX, N_GY, ORDER, BS), 1.0, 6.0, ((0, 32), (1, 16)), jnp.float32)
    start_front = draw_start_front(jax.random.fold_in(arg_keys[4], 71), 0)
    return dict(green=green, sources=sources, entering=entering, start_front=start_front)


def apply_row(operands):
    operator_row, rounded_row = operands
    return jnp.einsum("joi,jib->job", operator_row.astype(jnp.float32), rounded_row.astype(jnp.float32))


def reference(green, sources, entering, start_front):
    column_total = green.shape[0]
    row_total = green.shape[1]
    edge_rows = sources.shape[3]
    trace_rows = edge_rows // 2
    corner_rows = green.shape[2] - edge_rows
    width = entering.shape[3]
    front_map = (jnp.arange(column_total, dtype=jnp.int32)[:, None] + jnp.arange(row_total, dtype=jnp.int32)[None, :])
    incoming = entering
    traces = entering
    for step_index in range(TICKS):
        if step_index > 0:
            east_part = traces[:, :, :trace_rows]
            north_part = traces[:, :, trace_rows:edge_rows]
            corner_part = traces[:, :, edge_rows:]
            west_in = jnp.pad(east_part, ((1, 0), (0, 0), (0, 0), (0, 0)))[:-1]
            south_in = jnp.pad(north_part, ((0, 0), (1, 0), (0, 0), (0, 0)))[:, :-1]
            diagonal = jnp.pad(corner_part, ((1, 0), (1, 0), (0, 0), (0, 0)))[:-1, :-1]
            incoming = jnp.concatenate([west_in, south_in, diagonal], axis=2)
        rounded = incoming.astype(jnp.bfloat16)
        product = lax.map(apply_row, (green, rounded))
        source_term = jnp.concatenate([sources[step_index].astype(jnp.float32), jnp.zeros((column_total, row_total, corner_rows, width), jnp.float32)], axis=2)
        is_live = jnp.any(start_front[None, None, :] == (front_map - step_index)[:, :, None], axis=-1)
        traces = jnp.where(is_live[:, :, None, None], product + source_term, jnp.zeros_like(product))
    return traces
```

```python
import jax
import jax.numpy as jnp
from jax import lax
from jax.experimental import pallas as pl
from jax.experimental.pallas import tpu as pltpu
from jax.sharding import PartitionSpec as P

MESH = pl.DeviceIdType.MESH
LANES = 128
HALVES = 2
TILE = 256


def sweep_kernel(
    ticks, order, trace, width,
    fronts, green, sources, entering, last,
    operator, turned, source_rows, source_cols, first_in, sent, landed, held_half, result,
    green_sem, source_sem, entering_sem, last_sem, send_sem, land_sem,
):
    gx, gy = lax.axis_index("gx"), lax.axis_index("gy")
    columns, rows = lax.axis_size("gx"), lax.axis_size("gy")
    edge = 2 * trace
    half = width // HALVES
    blocks = order // LANES
    parts = (
        ("north", trace // LANES, edge // LANES, 0, 1),
        ("corner", edge // LANES, blocks, 1, 1),
        ("east", 0, trace // LANES, 1, 0),
    )
    tiles = [start for start in range(0, order, TILE)]
    tiles = [s for s in tiles if s + TILE > trace] + [s for s in tiles if s + TILE <= trace]

    def goes(dx, dy):
        ok = jnp.bool_(True)
        if dx:
            ok = jnp.logical_and(ok, gx < columns - 1)
        if dy:
            ok = jnp.logical_and(ok, gy < rows - 1)
        return ok

    def comes(dx, dy):
        ok = jnp.bool_(True)
        if dx:
            ok = jnp.logical_and(ok, gx > 0)
        if dy:
            ok = jnp.logical_and(ok, gy > 0)
        return ok

    barrier = pltpu.get_barrier_semaphore()
    for _, _, _, dx, dy in parts:
        @pl.when(comes(dx, dy))
        def _(dx=dx, dy=dy):
            pl.semaphore_signal(barrier, inc=1, device_id=(gx - dx, gy - dy), device_id_type=MESH)

    enter_copy = pltpu.make_async_copy(entering.at[0, 0], first_in, entering_sem)
    enter_copy.start()
    green_copies = {}
    for index, start in enumerate(tiles):
        copy = pltpu.make_async_copy(
            green.at[0, 0, pl.ds(start, TILE)], operator.at[pl.ds(start, TILE)], green_sem.at[index]
        )
        copy.start()
        green_copies[start] = copy
    source_copies = []
    for tick in range(ticks):
        copy = pltpu.make_async_copy(sources.at[tick, 0, 0], source_rows.at[tick], source_sem.at[tick])
        copy.start()
        source_copies.append(copy)

    for _, low, high, dx, dy in parts:
        @pl.when(jnp.logical_not(comes(dx, dy)))
        def _(low=low, high=high):
            landed[:, :, pl.ds(low, high - low)] = jnp.zeros(
                (ticks - 1, HALVES, high - low, half, LANES), jnp.bfloat16
            )

    def live_factor(tick):
        front = gx + gy - tick
        met = jnp.int32(0)
        for b in range(fronts.shape[0]):
            met = met | (fronts[b] == front).astype(jnp.int32)
        return met.astype(jnp.float32)

    def transfer(tick, h, index):
        _, low, high, dx, dy = parts[index]
        return pltpu.make_async_remote_copy(
            src_ref=sent.at[tick, h, pl.ds(low, high - low)],
            dst_ref=landed.at[tick, h, pl.ds(low, high - low)],
            send_sem=send_sem.at[tick, h, index],
            recv_sem=land_sem.at[tick, h, index],
            device_id=(gx + dx, gy + dy),
            device_id_type=MESH,
        )

    def send(tick, h, index):
        @pl.when(goes(*parts[index][3:]))
        def _():
            transfer(tick, h, index).start()

    def arrive(tick, h):
        for index in range(len(parts)):
            @pl.when(comes(*parts[index][3:]))
            def _(index=index):
                transfer(tick, h, index).wait_recv()

    def send_ready(tick, h, done):
        for index, (_, low, high, _, _) in enumerate(parts):
            if index not in done[1] and all(b in done[0] for b in range(low, high)):
                send(tick, h, index)
                done[1].add(index)

    enter_copy.wait()
    rounded = first_in[...].astype(jnp.bfloat16)
    live = live_factor(0)
    source_copies[0].wait()
    done = (set(), set())
    waited = False
    for start in tiles:
        green_copies[start].wait()
        product = jnp.dot(operator[start:start + TILE, :], rounded, preferred_element_type=jnp.float32)
        if start < edge:
            product = product + source_rows[0, start:start + TILE, :].astype(jnp.float32)
        out = (product * live).astype(jnp.bfloat16).T
        for q in range(TILE // LANES):
            block = start // LANES + q
            for h in range(HALVES):
                sent[0, h, block] = out[h * half:(h + 1) * half, q * LANES:(q + 1) * LANES]
            done[0].add(block)
        if not waited and all(b in done[0] for b in range(parts[0][1], parts[0][2])):
            count = sum(goes(dx, dy).astype(jnp.int32) for _, _, _, dx, dy in parts)

            @pl.when(count > 0)
            def _():
                pl.semaphore_wait(barrier, count)
            waited = True
        if waited:
            send_ready(0, 0, done)
    for h in range(1, HALVES):
        for index in range(len(parts)):
            send(0, h, index)

    for start in tiles:
        turned[:, start:start + TILE] = operator[start:start + TILE, :].T
    for tick in range(1, ticks):
        source_copies[tick].wait()
        if tick < ticks - 1:
            source_cols[tick] = source_rows[tick].T

    for tick in range(1, ticks - 1):
        live = live_factor(tick)
        for h in range(HALVES):
            arrive(tick - 1, h)
            incoming = jnp.concatenate([landed[tick - 1, h, b] for b in range(blocks)], axis=1)
            done = (set(), set())
            for start in tiles:
                product = jnp.dot(incoming, turned[:, start:start + TILE], preferred_element_type=jnp.float32)
                if start < edge:
                    product = product + source_cols[
                        tick, h * half:(h + 1) * half, start:start + TILE
                    ].astype(jnp.float32)
                out = (product * live).astype(jnp.bfloat16)
                for q in range(TILE // LANES):
                    block = start // LANES + q
                    sent[tick, h, block] = out[:, q * LANES:(q + 1) * LANES]
                    done[0].add(block)
                send_ready(tick, h, done)

    tick = ticks - 1
    live = live_factor(tick)
    for h in range(HALVES):
        arrive(tick - 1, h)
        incoming = jnp.concatenate([landed[tick - 1, h, b] for b in range(blocks)], axis=1)
        for index, start in enumerate(tiles):
            product = jnp.dot(incoming, turned[:, start:start + TILE], preferred_element_type=jnp.float32)
            held_half[h * half:(h + 1) * half, start:start + TILE] = product
            if h == HALVES - 1:
                whole = held_half[:, start:start + TILE].T
                if start < edge:
                    whole = whole + source_rows[tick, start:start + TILE, :].astype(jnp.float32)
                result[start:start + TILE, :] = whole * live
                pltpu.make_async_copy(
                    result.at[pl.ds(start, TILE)], last.at[0, 0, pl.ds(start, TILE)], last_sem.at[index]
                ).start()
    for index, start in enumerate(tiles):
        pltpu.make_async_copy(
            result.at[pl.ds(start, TILE)], last.at[0, 0, pl.ds(start, TILE)], last_sem.at[index]
        ).wait()
    for tick in range(ticks - 1):
        for h in range(HALVES):
            for index in range(len(parts)):
                @pl.when(goes(*parts[index][3:]))
                def _(tick=tick, h=h, index=index):
                    transfer(tick, h, index).wait_send()


def local(green, sources, entering, start_front):
    ticks, edge = sources.shape[0], sources.shape[3]
    order, width = entering.shape[2], entering.shape[3]
    half, blocks = width // HALVES, order // LANES
    n_tiles = order // TILE

    def body(*refs):
        sweep_kernel(ticks, order, edge // 2, width, *refs)

    hbm = pl.BlockSpec(memory_space=pltpu.HBM)
    return pl.pallas_call(
        body,
        name="sweep",
        out_shape=jax.ShapeDtypeStruct(entering.shape, jnp.float32),
        in_specs=[pl.BlockSpec(memory_space=pltpu.SMEM), hbm, hbm, hbm],
        out_specs=hbm,
        scratch_shapes=[
            pltpu.VMEM((order, order), jnp.bfloat16),
            pltpu.VMEM((order, order), jnp.bfloat16),
            pltpu.VMEM((ticks, edge, width), jnp.bfloat16),
            pltpu.VMEM((ticks, width, edge), jnp.bfloat16),
            pltpu.VMEM((order, width), jnp.float32),
            pltpu.VMEM((ticks - 1, HALVES, blocks, half, LANES), jnp.bfloat16),
            pltpu.VMEM((ticks - 1, HALVES, blocks, half, LANES), jnp.bfloat16),
            pltpu.VMEM((width, order), jnp.float32),
            pltpu.VMEM((order, width), jnp.float32),
            pltpu.SemaphoreType.DMA((n_tiles,)),
            pltpu.SemaphoreType.DMA((ticks,)),
            pltpu.SemaphoreType.DMA,
            pltpu.SemaphoreType.DMA((n_tiles,)),
            pltpu.SemaphoreType.DMA((ticks - 1, HALVES, 3)),
            pltpu.SemaphoreType.DMA((ticks - 1, HALVES, 3)),
        ],
        compiler_params=pltpu.CompilerParams(
            collective_id=0, has_side_effects=True, vmem_limit_bytes=56 * 1024 * 1024
        ),
        cost_estimate=pl.CostEstimate(
            flops=2 * ticks * order * order * width,
            bytes_accessed=2 * order * order + 2 * ticks * edge * width + 8 * order * width,
            transcendentals=0,
        ),
    )(start_front, green, sources, entering)


def solution(mesh):
    in_specs = (
        P("gx", "gy", None, None),
        P(None, "gx", "gy", None, None),
        P("gx", "gy", None, None),
        P(),
    )
    out_specs = P("gx", "gy", None, None)
    return jax.shard_map(local, mesh=mesh, in_specs=in_specs, out_specs=out_specs, check_vma=False)
```

```python
import jax
import jax.numpy as jnp
from jax import lax
from jax.experimental import pallas as pl
from jax.experimental.pallas import tpu as pltpu
from jax.sharding import PartitionSpec as P

MESH = pl.DeviceIdType.MESH
LANES = 128
CHUNKS = 4
TILE = 256


def sweep_kernel(
    ticks, order, trace, width,
    fronts_hbm, green, sources, entering, last,
    fronts, operator, turned, source_rows, source_cols, first_in, sent, landed, held_chunk, zeros,
    front_sem, green_sem, source_sem, entering_sem, send_sem, land_sem,
):
    gx, gy = lax.axis_index("gx"), lax.axis_index("gy")
    columns, rows = lax.axis_size("gx"), lax.axis_size("gy")
    edge = 2 * trace
    size = width // CHUNKS
    blocks = order // LANES
    parts = (
        (trace // LANES, edge // LANES, 0, 1),
        (edge // LANES, blocks, 1, 1),
        (0, trace // LANES, 1, 0),
    )
    tiles = [start for start in range(0, order, TILE)]
    tiles = [s for s in tiles if s + TILE > trace] + [s for s in tiles if s + TILE <= trace]

    def goes(dx, dy):
        ok = [gx < columns - 1] * dx + [gy < rows - 1] * dy
        return ok[0] if len(ok) == 1 else jnp.logical_and(*ok)

    def comes(dx, dy):
        ok = [gx > 0] * dx + [gy > 0] * dy
        return ok[0] if len(ok) == 1 else jnp.logical_and(*ok)

    barrier = pltpu.get_barrier_semaphore()
    for _, _, dx, dy in parts:
        @pl.when(comes(dx, dy))
        def _(dx=dx, dy=dy):
            pl.semaphore_signal(barrier, inc=1, device_id=(gx - dx, gy - dy), device_id_type=MESH)

    enter_copy = pltpu.make_async_copy(entering.at[0, 0], first_in, entering_sem)
    front_copy = pltpu.make_async_copy(fronts_hbm, fronts, front_sem)
    green_copies = {
        start: pltpu.make_async_copy(
            green.at[0, 0, pl.ds(start, TILE)], operator.at[pl.ds(start, TILE)], green_sem.at[index]
        )
        for index, start in enumerate(tiles)
    }
    source_copies = [
        pltpu.make_async_copy(sources.at[tick, 0, 0], source_rows.at[tick], source_sem.at[tick])
        for tick in range(ticks)
    ]
    enter_copy.start()
    green_copies[tiles[0]].start()
    front_copy.start()
    source_copies[0].start()
    for start in tiles[1:]:
        green_copies[start].start()
    for tick in range(1, ticks):
        source_copies[tick].start()

    def live_factor(tick):
        front = gx + gy - tick
        met = jnp.int32(0)
        for b in range(fronts.shape[0]):
            met = met | (fronts[b] == front).astype(jnp.int32)
        return met.astype(jnp.float32)

    zeros[...] = jnp.zeros(zeros.shape, jnp.bfloat16)
    for low, high, dx, dy in parts:
        @pl.when(jnp.logical_not(comes(dx, dy)))
        def _(low=low, high=high):
            for tick in range(ticks - 1):
                for h in range(CHUNKS):
                    pltpu.make_async_copy(
                        zeros.at[pl.ds(0, high - low)], landed.at[tick, h, pl.ds(low, high - low)],
                        land_sem.at[tick, h],
                    ).start()

    def transfer(tick, h, index):
        low, high, dx, dy = parts[index]
        return pltpu.make_async_remote_copy(
            src_ref=sent.at[tick, h, pl.ds(low, high - low)],
            dst_ref=landed.at[tick, h, pl.ds(low, high - low)],
            send_sem=send_sem.at[index],
            recv_sem=land_sem.at[tick, h],
            device_id=(gx + dx, gy + dy),
            device_id_type=MESH,
        )

    def send(tick, h, index):
        @pl.when(goes(*parts[index][2:]))
        def _():
            transfer(tick, h, index).start()

    def arrive(tick, h):
        pltpu.make_async_copy(landed.at[tick, h], landed.at[tick, h], land_sem.at[tick, h]).wait()

    def send_ready(tick, h, done):
        for index, (low, high, _, _) in enumerate(parts):
            if index not in done[1] and all(b in done[0] for b in range(low, high)):
                send(tick, h, index)
                done[1].add(index)

    enter_copy.wait()
    rounded = first_in[...].astype(jnp.bfloat16)
    front_copy.wait()
    live = live_factor(0)
    source_copies[0].wait()
    done = (set(), set())
    waited = False
    for start in tiles:
        green_copies[start].wait()
        product = jnp.dot(operator[start:start + TILE, :], rounded, preferred_element_type=jnp.float32)
        if start < edge:
            product = product + source_rows[0, start:start + TILE, :].astype(jnp.float32)
        out = (product * live).astype(jnp.bfloat16).T
        for q in range(TILE // LANES):
            block = start // LANES + q
            for h in range(CHUNKS):
                sent[0, h, block] = out[h * size:(h + 1) * size, q * LANES:(q + 1) * LANES]
            done[0].add(block)
        if not waited and all(b in done[0] for b in range(parts[0][0], parts[0][1])):
            count = sum(goes(dx, dy).astype(jnp.int32) for _, _, dx, dy in parts)

            @pl.when(count > 0)
            def _():
                pl.semaphore_wait(barrier, count)
            waited = True
        if waited:
            send_ready(0, 0, done)
    for h in range(1, CHUNKS):
        for index in range(len(parts)):
            send(0, h, index)

    for start in tiles:
        turned[:, start:start + TILE] = operator[start:start + TILE, :].T

    for tick in range(1, ticks):
        source_copies[tick].wait()
        if tick < ticks - 1:
            source_cols[tick] = source_rows[tick].T

    for tick in range(1, ticks - 1):
        live = live_factor(tick)
        for h in range(CHUNKS):
            arrive(tick - 1, h)
            incoming = jnp.concatenate([landed[tick - 1, h, b] for b in range(blocks)], axis=1)
            done = (set(), set())
            for start in tiles:
                product = jnp.dot(incoming, turned[:, start:start + TILE], preferred_element_type=jnp.float32)
                if start < edge:
                    product = product + source_cols[
                        tick, h * size:(h + 1) * size, start:start + TILE
                    ].astype(jnp.float32)
                out = (product * live).astype(jnp.bfloat16)
                for q in range(TILE // LANES):
                    block = start // LANES + q
                    sent[tick, h, block] = out[:, q * LANES:(q + 1) * LANES]
                    done[0].add(block)
                send_ready(tick, h, done)

    tick = ticks - 1
    live = live_factor(tick)
    for h in range(CHUNKS):
        if h == CHUNKS - 1:
            for index, (low, high, dx, dy) in enumerate(parts):
                @pl.when(goes(dx, dy))
                def _(low=low, high=high, index=index):
                    whole = sent.at[:, :, pl.ds(low, high - low)]
                    pltpu.make_async_copy(whole, whole, send_sem.at[index]).wait()
        arrive(tick - 1, h)
        incoming = jnp.concatenate([landed[tick - 1, h, b] for b in range(blocks)], axis=1)
        for start in tiles:
            product = jnp.dot(incoming, turned[:, start:start + TILE], preferred_element_type=jnp.float32)
            if h < CHUNKS - 1:
                held_chunk[h * size:(h + 1) * size, start:start + TILE] = product
            else:
                held = held_chunk[:, start:start + TILE]
                whole = jnp.concatenate([held, product], axis=0).T
                if start < edge:
                    whole = whole + source_rows[tick, start:start + TILE, :].astype(jnp.float32)
                last[0, 0, start:start + TILE, :] = whole * live


def local(green, sources, entering, start_front):
    ticks, edge = sources.shape[0], sources.shape[3]
    order, width = entering.shape[2], entering.shape[3]
    size, blocks = width // CHUNKS, order // LANES
    n_tiles = order // TILE

    def body(*refs):
        sweep_kernel(ticks, order, edge // 2, width, *refs)

    hbm = pl.BlockSpec(memory_space=pltpu.HBM)
    return pl.pallas_call(
        body,
        name="sweep",
        out_shape=jax.ShapeDtypeStruct(entering.shape, jnp.float32),
        in_specs=[hbm, hbm, hbm, hbm],
        out_specs=pl.BlockSpec(memory_space=pltpu.VMEM),
        scratch_shapes=[
            pltpu.SMEM(start_front.shape, jnp.int32),
            pltpu.VMEM((order, order), jnp.bfloat16),
            pltpu.VMEM((order, order), jnp.bfloat16),
            pltpu.VMEM((ticks, edge, width), jnp.bfloat16),
            pltpu.VMEM((ticks, width, edge), jnp.bfloat16),
            pltpu.VMEM((order, width), jnp.float32),
            pltpu.VMEM((ticks - 1, CHUNKS, blocks, size, LANES), jnp.bfloat16),
            pltpu.VMEM((ticks - 1, CHUNKS, blocks, size, LANES), jnp.bfloat16),
            pltpu.VMEM((width - size, order), jnp.float32),
            pltpu.VMEM((edge // 2 // LANES, size, LANES), jnp.bfloat16),
            pltpu.SemaphoreType.DMA,
            pltpu.SemaphoreType.DMA((n_tiles,)),
            pltpu.SemaphoreType.DMA((ticks,)),
            pltpu.SemaphoreType.DMA,
            pltpu.SemaphoreType.DMA((3,)),
            pltpu.SemaphoreType.DMA((ticks - 1, CHUNKS)),
        ],
        compiler_params=pltpu.CompilerParams(
            collective_id=0, has_side_effects=True, vmem_limit_bytes=54600 * 1024
        ),
        cost_estimate=pl.CostEstimate(
            flops=2 * ticks * order * order * width,
            bytes_accessed=2 * order * order + 2 * ticks * edge * width + 8 * order * width,
            transcendentals=0,
        ),
    )(start_front, green, sources, entering)


def solution(mesh):
    in_specs = (
        P("gx", "gy", None, None),
        P(None, "gx", "gy", None, None),
        P("gx", "gy", None, None),
        P(),
    )
    out_specs = P("gx", "gy", None, None)
    return jax.shard_map(local, mesh=mesh, in_specs=in_specs, out_specs=out_specs, check_vma=False)
```

```python
import jax
import jax.numpy as jnp
from jax import lax
from jax.experimental import pallas as pl
from jax.experimental.pallas import tpu as pltpu
from jax.sharding import PartitionSpec as P

MESH = pl.DeviceIdType.MESH
LANES = 128
CHUNKS = (32, 32, 32, 32)
TILE = 256


def sweep_kernel(
    ticks, order, trace, width,
    fronts_hbm, green, sources, entering, last,
    fronts, operator, turned, source_rows, source_cols, first_in, sent, landed, held_chunk, zeros,
    front_sem, green_sem, source_sem, entering_sem, send_sem, land_sem,
):
    gx, gy = lax.axis_index("gx"), lax.axis_index("gy")
    columns, rows = lax.axis_size("gx"), lax.axis_size("gy")
    edge = 2 * trace
    offsets = [sum(CHUNKS[:h]) for h in range(len(CHUNKS))]
    final = len(CHUNKS) - 1
    blocks = order // LANES
    parts = (
        (trace // LANES, edge // LANES, 0, 1),
        (edge // LANES, blocks, 1, 1),
        (0, trace // LANES, 1, 0),
    )
    tiles = [start for start in range(0, order, TILE)]
    tiles = [s for s in tiles if s + TILE > trace] + [s for s in tiles if s + TILE <= trace]

    def goes(dx, dy):
        ok = [gx < columns - 1] * dx + [gy < rows - 1] * dy
        return ok[0] if len(ok) == 1 else jnp.logical_and(*ok)

    def comes(dx, dy):
        ok = [gx > 0] * dx + [gy > 0] * dy
        return ok[0] if len(ok) == 1 else jnp.logical_and(*ok)

    barrier = pltpu.get_barrier_semaphore()
    for _, _, dx, dy in parts:
        @pl.when(comes(dx, dy))
        def _(dx=dx, dy=dy):
            pl.semaphore_signal(barrier, inc=1, device_id=(gx - dx, gy - dy), device_id_type=MESH)

    enter_copy = pltpu.make_async_copy(entering.at[0, 0], first_in, entering_sem)
    front_copy = pltpu.make_async_copy(fronts_hbm, fronts, front_sem)
    green_copies = {
        start: pltpu.make_async_copy(
            green.at[0, 0, pl.ds(start, TILE)], operator.at[pl.ds(start, TILE)], green_sem.at[index]
        )
        for index, start in enumerate(tiles)
    }
    source_copies = [
        pltpu.make_async_copy(sources.at[tick, 0, 0], source_rows.at[tick], source_sem.at[tick])
        for tick in range(ticks)
    ]
    enter_copy.start()
    green_copies[tiles[0]].start()
    front_copy.start()
    source_copies[0].start()
    for start in tiles[1:]:
        green_copies[start].start()
    for tick in range(1, ticks):
        source_copies[tick].start()

    def live_factor(tick):
        front = gx + gy - tick
        met = jnp.int32(0)
        for b in range(fronts.shape[0]):
            met = met | (fronts[b] == front).astype(jnp.int32)
        return met.astype(jnp.float32)

    def place(h, low, high):
        return pl.ds(offsets[h] * blocks + low * CHUNKS[h], (high - low) * CHUNKS[h])

    zeros[...] = jnp.zeros(zeros.shape, jnp.bfloat16)
    for low, high, dx, dy in parts:
        @pl.when(jnp.logical_not(comes(dx, dy)))
        def _(low=low, high=high):
            for tick in range(ticks - 1):
                for h, size in enumerate(CHUNKS):
                    pltpu.make_async_copy(
                        zeros.at[pl.ds(0, (high - low) * size)], landed.at[tick, place(h, low, high)],
                        land_sem.at[tick, h],
                    ).start()

    def transfer(tick, h, index):
        low, high, dx, dy = parts[index]
        return pltpu.make_async_remote_copy(
            src_ref=sent.at[tick, place(h, low, high)],
            dst_ref=landed.at[tick, place(h, low, high)],
            send_sem=send_sem.at[index],
            recv_sem=land_sem.at[tick, h],
            device_id=(gx + dx, gy + dy),
            device_id_type=MESH,
        )

    def send(tick, h, index):
        @pl.when(goes(*parts[index][2:]))
        def _():
            transfer(tick, h, index).start()

    def arrive(tick, h):
        whole = landed.at[tick, place(h, 0, blocks)]
        pltpu.make_async_copy(whole, whole, land_sem.at[tick, h]).wait()

    def send_ready(tick, h, done):
        for index, (low, high, _, _) in enumerate(parts):
            if index not in done[1] and all(b in done[0] for b in range(low, high)):
                send(tick, h, index)
                done[1].add(index)

    enter_copy.wait()
    rounded = first_in[...].astype(jnp.bfloat16)
    front_copy.wait()
    live = live_factor(0)
    source_copies[0].wait()
    done = (set(), set())
    waited = False
    for start in tiles:
        green_copies[start].wait()
        product = jnp.dot(operator[start:start + TILE, :], rounded, preferred_element_type=jnp.float32)
        if start < edge:
            product = product + source_rows[0, start:start + TILE, :].astype(jnp.float32)
        out = (product * live).astype(jnp.bfloat16).T
        for q in range(TILE // LANES):
            block = start // LANES + q
            for h, size in enumerate(CHUNKS):
                sent[0, place(h, block, block + 1)] = out[
                    offsets[h]:offsets[h] + size, q * LANES:(q + 1) * LANES
                ]
            done[0].add(block)
        if not waited and all(b in done[0] for b in range(parts[0][0], parts[0][1])):
            count = sum(goes(dx, dy).astype(jnp.int32) for _, _, dx, dy in parts)

            @pl.when(count > 0)
            def _():
                pl.semaphore_wait(barrier, count)
            waited = True
        if waited:
            send_ready(0, 0, done)
    for index in range(len(parts)):
        for h in range(1, len(CHUNKS)):
            send(0, h, index)

    for start in tiles:
        turned[:, start:start + TILE] = operator[start:start + TILE, :].T

    for tick in range(1, ticks):
        source_copies[tick].wait()
        if tick < ticks - 1:
            source_cols[tick] = source_rows[tick].T

    for tick in range(1, ticks - 1):
        live = live_factor(tick)
        for h, size in enumerate(CHUNKS):
            arrive(tick - 1, h)
            incoming = jnp.concatenate([landed[tick - 1, place(h, b, b + 1)] for b in range(blocks)], axis=1)
            done = (set(), set())
            for start in tiles:
                product = jnp.dot(incoming, turned[:, start:start + TILE], preferred_element_type=jnp.float32)
                if start < edge:
                    product = product + source_cols[
                        tick, offsets[h]:offsets[h] + size, start:start + TILE
                    ].astype(jnp.float32)
                out = (product * live).astype(jnp.bfloat16)
                for q in range(TILE // LANES):
                    block = start // LANES + q
                    sent[tick, place(h, block, block + 1)] = out[:, q * LANES:(q + 1) * LANES]
                    done[0].add(block)
                send_ready(tick, h, done)

    tick = ticks - 1
    live = live_factor(tick)
    for h, size in enumerate(CHUNKS):
        if h == final:
            for index, (low, high, dx, dy) in enumerate(parts):
                @pl.when(goes(dx, dy))
                def _(low=low, high=high, index=index):
                    whole = sent.at[:, pl.ds(0, (high - low) * width)]
                    pltpu.make_async_copy(whole, whole, send_sem.at[index]).wait()
        arrive(tick - 1, h)
        incoming = jnp.concatenate([landed[tick - 1, place(h, b, b + 1)] for b in range(blocks)], axis=1)
        for start in tiles:
            product = jnp.dot(incoming, turned[:, start:start + TILE], preferred_element_type=jnp.float32)
            if h < final:
                held_chunk[offsets[h]:offsets[h] + size, start:start + TILE] = product
            else:
                held = held_chunk[:, start:start + TILE]
                whole = jnp.concatenate([held, product], axis=0).T
                if start < edge:
                    whole = whole + source_rows[tick, start:start + TILE, :].astype(jnp.float32)
                last[0, 0, start:start + TILE, :] = whole * live


def local(green, sources, entering, start_front):
    ticks, edge = sources.shape[0], sources.shape[3]
    order, width = entering.shape[2], entering.shape[3]
    blocks = order // LANES
    n_tiles = order // TILE

    def body(*refs):
        sweep_kernel(ticks, order, edge // 2, width, *refs)

    hbm = pl.BlockSpec(memory_space=pltpu.HBM)
    return pl.pallas_call(
        body,
        name="sweep",
        out_shape=jax.ShapeDtypeStruct(entering.shape, jnp.float32),
        in_specs=[hbm, hbm, hbm, hbm],
        out_specs=pl.BlockSpec(memory_space=pltpu.VMEM),
        scratch_shapes=[
            pltpu.SMEM(start_front.shape, jnp.int32),
            pltpu.VMEM((order, order), jnp.bfloat16),
            pltpu.VMEM((order, order), jnp.bfloat16),
            pltpu.VMEM((ticks, edge, width), jnp.bfloat16),
            pltpu.VMEM((ticks, width, edge), jnp.bfloat16),
            pltpu.VMEM((order, width), jnp.float32),
            pltpu.VMEM((ticks - 1, blocks * width, LANES), jnp.bfloat16),
            pltpu.VMEM((ticks - 1, blocks * width, LANES), jnp.bfloat16),
            pltpu.VMEM((width - CHUNKS[-1], order), jnp.float32),
            pltpu.VMEM((edge // 2 // LANES * max(CHUNKS), LANES), jnp.bfloat16),
            pltpu.SemaphoreType.DMA,
            pltpu.SemaphoreType.DMA((n_tiles,)),
            pltpu.SemaphoreType.DMA((ticks,)),
            pltpu.SemaphoreType.DMA,
            pltpu.SemaphoreType.DMA((3,)),
            pltpu.SemaphoreType.DMA((ticks - 1, len(CHUNKS))),
        ],
        compiler_params=pltpu.CompilerParams(
            collective_id=0, has_side_effects=True, vmem_limit_bytes=32 * 1024 * 1024
        ),
        cost_estimate=pl.CostEstimate(
            flops=2 * ticks * order * order * width,
            bytes_accessed=2 * order * order + 2 * ticks * edge * width + 8 * order * width,
            transcendentals=0,
        ),
    )(*(pltpu.with_memory_space_constraint(a, pltpu.HBM) for a in (start_front, green, sources, entering)))


def solution(mesh):
    in_specs = (
        P("gx", "gy", None, None),
        P(None, "gx", "gy", None, None),
        P("gx", "gy", None, None),
        P(),
    )
    out_specs = P("gx", "gy", None, None)
    return jax.shard_map(local, mesh=mesh, in_specs=in_specs, out_specs=out_specs, check_vma=False)
```

```python
import jax
import jax.numpy as jnp
from jax import lax
from jax.experimental import pallas as pl
from jax.experimental.pallas import tpu as pltpu
from jax.sharding import PartitionSpec as P

MESH = pl.DeviceIdType.MESH
LANES = 128
CHUNKS = (32, 32, 32, 32)
TILE = 256


def sweep_kernel(
    ticks, order, trace, width,
    fronts_hbm, green, sources, entering, last,
    fronts, operator, turned, source_rows, source_cols, first_in, sent, landed, held_chunk, zeros,
    front_sem, green_sem, source_sem, entering_sem, send_sem, land_sem,
):
    gx, gy = lax.axis_index("gx"), lax.axis_index("gy")
    columns, rows = lax.axis_size("gx"), lax.axis_size("gy")
    edge = 2 * trace
    offsets = [sum(CHUNKS[:h]) for h in range(len(CHUNKS))]
    final = len(CHUNKS) - 1
    blocks = order // LANES
    parts = (
        (trace // LANES, edge // LANES, 0, 1),
        (edge // LANES, blocks, 1, 1),
        (0, trace // LANES, 1, 0),
    )
    tiles = [start for start in range(0, order, TILE)]
    tiles = [s for s in tiles if s + TILE > trace] + [s for s in tiles if s + TILE <= trace]

    def goes(dx, dy):
        ok = [gx < columns - 1] * dx + [gy < rows - 1] * dy
        return ok[0] if len(ok) == 1 else jnp.logical_and(*ok)

    def comes(dx, dy):
        ok = [gx > 0] * dx + [gy > 0] * dy
        return ok[0] if len(ok) == 1 else jnp.logical_and(*ok)

    to_next = [goes(dx, dy) for _, _, dx, dy in parts]
    next_device = [(gx + dx, gy + dy) for _, _, dx, dy in parts]

    barrier = pltpu.get_barrier_semaphore()
    for _, _, dx, dy in parts:
        @pl.when(comes(dx, dy))
        def _(dx=dx, dy=dy):
            pl.semaphore_signal(barrier, inc=1, device_id=(gx - dx, gy - dy), device_id_type=MESH)

    enter_copy = pltpu.make_async_copy(entering.at[0, 0], first_in, entering_sem)
    front_copy = pltpu.make_async_copy(fronts_hbm, fronts, front_sem)
    green_copies = {
        start: pltpu.make_async_copy(
            green.at[0, 0, pl.ds(start, TILE)], operator.at[pl.ds(start, TILE)], green_sem.at[index]
        )
        for index, start in enumerate(tiles)
    }
    source_copies = [
        pltpu.make_async_copy(sources.at[tick, 0, 0], source_rows.at[tick], source_sem.at[tick])
        for tick in range(ticks)
    ]
    enter_copy.start()
    green_copies[tiles[0]].start()
    front_copy.start()
    source_copies[0].start()
    for start in tiles[1:]:
        green_copies[start].start()
    for tick in range(1, ticks):
        source_copies[tick].start()

    def live_factor(tick):
        front = gx + gy - tick
        met = jnp.int32(0)
        for b in range(fronts.shape[0]):
            met = met | (fronts[b] == front).astype(jnp.int32)
        return met.astype(jnp.float32)

    def place(h, low, high):
        return pl.ds(offsets[h] * blocks + low * CHUNKS[h], (high - low) * CHUNKS[h])

    zeros[...] = jnp.zeros(zeros.shape, jnp.bfloat16)
    for low, high, dx, dy in parts:
        @pl.when(jnp.logical_not(comes(dx, dy)))
        def _(low=low, high=high):
            for tick in range(ticks - 1):
                for h, size in enumerate(CHUNKS):
                    pltpu.make_async_copy(
                        zeros.at[pl.ds(0, (high - low) * size)], landed.at[tick, place(h, low, high)],
                        land_sem.at[tick, h],
                    ).start()

    def transfer(tick, h, index):
        low, high, _, _ = parts[index]
        return pltpu.make_async_remote_copy(
            src_ref=sent.at[tick, place(h, low, high)],
            dst_ref=landed.at[tick, place(h, low, high)],
            send_sem=send_sem.at[index],
            recv_sem=land_sem.at[tick, h],
            device_id=next_device[index],
            device_id_type=MESH,
        )

    def send(tick, h, index):
        ok = to_next[index]
        if index == 0:
            @pl.when(jnp.logical_and(ok, gx % 2 == 0))
            def _():
                transfer(tick, h, index).start()
        else:
            @pl.when(ok)
            def _():
                transfer(tick, h, index).start()
        if index == 1:
            @pl.when(jnp.logical_and(goes(0, 1), gx % 2 == 1))
            def _():
                transfer(tick, h, 0).start()

    def arrive(tick, h):
        whole = landed.at[tick, place(h, 0, blocks)]
        pltpu.make_async_copy(whole, whole, land_sem.at[tick, h]).wait()

    def send_ready(tick, h, done):
        for index, (low, high, _, _) in enumerate(parts):
            if index not in done[1] and all(b in done[0] for b in range(low, high)):
                send(tick, h, index)
                done[1].add(index)

    enter_copy.wait()
    rounded = first_in[...].astype(jnp.bfloat16)
    front_copy.wait()
    live = live_factor(0)
    source_copies[0].wait()
    done = (set(), set())
    waited = False
    for start in tiles:
        green_copies[start].wait()
        product = jnp.dot(operator[start:start + TILE, :], rounded, preferred_element_type=jnp.float32)
        if start < edge:
            product = product + source_rows[0, start:start + TILE, :].astype(jnp.float32)
        out = (product * live).astype(jnp.bfloat16).T
        for q in range(TILE // LANES):
            block = start // LANES + q
            for h, size in enumerate(CHUNKS):
                sent[0, place(h, block, block + 1)] = out[
                    offsets[h]:offsets[h] + size, q * LANES:(q + 1) * LANES
                ]
            done[0].add(block)
        if not waited and all(b in done[0] for b in range(parts[0][0], parts[0][1])):
            count = sum(goes(dx, dy).astype(jnp.int32) for _, _, dx, dy in parts)

            @pl.when(count > 0)
            def _():
                pl.semaphore_wait(barrier, count)
            waited = True
        if waited:
            send_ready(0, 0, done)
    for index in range(len(parts)):
        for h in range(1, len(CHUNKS)):
            send(0, h, index)

    for start in tiles:
        turned[:, start:start + TILE] = operator[start:start + TILE, :].T

    for tick in range(1, ticks):
        source_copies[tick].wait()
        if tick < ticks - 1:
            source_cols[tick] = source_rows[tick].T

    for tick in range(1, ticks - 1):
        live = live_factor(tick)
        for h, size in enumerate(CHUNKS):
            arrive(tick - 1, h)
            incoming = jnp.concatenate([landed[tick - 1, place(h, b, b + 1)] for b in range(blocks)], axis=1)
            done = (set(), set())
            for start in tiles:
                product = jnp.dot(incoming, turned[:, start:start + TILE], preferred_element_type=jnp.float32)
                if start < edge:
                    product = product + source_cols[
                        tick, offsets[h]:offsets[h] + size, start:start + TILE
                    ].astype(jnp.float32)
                out = (product * live).astype(jnp.bfloat16)
                for q in range(TILE // LANES):
                    block = start // LANES + q
                    sent[tick, place(h, block, block + 1)] = out[:, q * LANES:(q + 1) * LANES]
                    done[0].add(block)
                send_ready(tick, h, done)

    tick = ticks - 1
    live = live_factor(tick)
    for h, size in enumerate(CHUNKS):
        if h == final:
            for index, (low, high, dx, dy) in enumerate(parts):
                @pl.when(goes(dx, dy))
                def _(low=low, high=high, index=index):
                    whole = sent.at[:, pl.ds(0, (high - low) * width)]
                    pltpu.make_async_copy(whole, whole, send_sem.at[index]).wait()
        arrive(tick - 1, h)
        incoming = jnp.concatenate([landed[tick - 1, place(h, b, b + 1)] for b in range(blocks)], axis=1)
        for start in tiles:
            product = jnp.dot(incoming, turned[:, start:start + TILE], preferred_element_type=jnp.float32)
            if h < final:
                held_chunk[offsets[h]:offsets[h] + size, start:start + TILE] = product
            else:
                held = held_chunk[:, start:start + TILE]
                whole = jnp.concatenate([held, product], axis=0).T
                if start < edge:
                    whole = whole + source_rows[tick, start:start + TILE, :].astype(jnp.float32)
                last[0, 0, start:start + TILE, :] = whole * live


def local(green, sources, entering, start_front):
    ticks, edge = sources.shape[0], sources.shape[3]
    order, width = entering.shape[2], entering.shape[3]
    blocks = order // LANES
    n_tiles = order // TILE

    def body(*refs):
        sweep_kernel(ticks, order, edge // 2, width, *refs)

    hbm = pl.BlockSpec(memory_space=pltpu.HBM)
    return pl.pallas_call(
        body,
        name="sweep",
        out_shape=jax.ShapeDtypeStruct(entering.shape, jnp.float32),
        in_specs=[hbm, hbm, hbm, hbm],
        out_specs=pl.BlockSpec(memory_space=pltpu.VMEM),
        scratch_shapes=[
            pltpu.SMEM(start_front.shape, jnp.int32),
            pltpu.VMEM((order, order), jnp.bfloat16),
            pltpu.VMEM((order, order), jnp.bfloat16),
            pltpu.VMEM((ticks, edge, width), jnp.bfloat16),
            pltpu.VMEM((ticks, width, edge), jnp.bfloat16),
            pltpu.VMEM((order, width), jnp.float32),
            pltpu.VMEM((ticks - 1, blocks * width, LANES), jnp.bfloat16),
            pltpu.VMEM((ticks - 1, blocks * width, LANES), jnp.bfloat16),
            pltpu.VMEM((width - CHUNKS[-1], order), jnp.float32),
            pltpu.VMEM((edge // 2 // LANES * max(CHUNKS), LANES), jnp.bfloat16),
            pltpu.SemaphoreType.DMA,
            pltpu.SemaphoreType.DMA((n_tiles,)),
            pltpu.SemaphoreType.DMA((ticks,)),
            pltpu.SemaphoreType.DMA,
            pltpu.SemaphoreType.DMA((3,)),
            pltpu.SemaphoreType.DMA((ticks - 1, len(CHUNKS))),
        ],
        compiler_params=pltpu.CompilerParams(
            collective_id=0, has_side_effects=True, vmem_limit_bytes=32 * 1024 * 1024
        ),
        cost_estimate=pl.CostEstimate(
            flops=2 * ticks * order * order * width,
            bytes_accessed=2 * order * order + 2 * ticks * edge * width + 8 * order * width,
            transcendentals=0,
        ),
    )(*(pltpu.with_memory_space_constraint(a, pltpu.HBM) for a in (start_front, green, sources, entering)))


def solution(mesh):
    in_specs = (
        P("gx", "gy", None, None),
        P(None, "gx", "gy", None, None),
        P("gx", "gy", None, None),
        P(),
    )
    out_specs = P("gx", "gy", None, None)
    return jax.shard_map(local, mesh=mesh, in_specs=in_specs, out_specs=out_specs, check_vma=False)
```

```python
import jax
import jax.numpy as jnp
from jax import lax
from jax.experimental import pallas as pl
from jax.experimental.pallas import tpu as pltpu
from jax.sharding import PartitionSpec as P

MESH = pl.DeviceIdType.MESH
LANES = 128
CHUNKS = (32, 32, 32, 32)
TILE = 256


def sweep_kernel(
    ticks, order, trace, width,
    fronts_hbm, green, sources, entering, last,
    fronts, operator, turned, source_rows, source_cols, first_in, sent, landed, held_chunk, zeros,
    front_sem, green_sem, source_sem, entering_sem, send_sem, land_sem,
):
    gx, gy = lax.axis_index("gx"), lax.axis_index("gy")
    columns, rows = lax.axis_size("gx"), lax.axis_size("gy")
    edge = 2 * trace
    offsets = [sum(CHUNKS[:h]) for h in range(len(CHUNKS))]
    final = len(CHUNKS) - 1
    blocks = order // LANES
    parts = (
        (trace // LANES, edge // LANES, 0, 1),
        (edge // LANES, blocks, 1, 1),
        (0, trace // LANES, 1, 0),
    )
    tiles = [start for start in range(0, order, TILE)]
    tiles = [s for s in tiles if s + TILE > trace] + [s for s in tiles if s + TILE <= trace]

    def goes(dx, dy):
        ok = [gx < columns - 1] * dx + [gy < rows - 1] * dy
        return ok[0] if len(ok) == 1 else jnp.logical_and(*ok)

    def comes(dx, dy):
        ok = [gx > 0] * dx + [gy > 0] * dy
        return ok[0] if len(ok) == 1 else jnp.logical_and(*ok)

    to_next = [goes(dx, dy) for _, _, dx, dy in parts]
    next_device = [(gx + dx, gy + dy) for _, _, dx, dy in parts]

    barrier = pltpu.get_barrier_semaphore()
    for _, _, dx, dy in parts:
        @pl.when(comes(dx, dy))
        def _(dx=dx, dy=dy):
            pl.semaphore_signal(barrier, inc=1, device_id=(gx - dx, gy - dy), device_id_type=MESH)

    enter_copy = pltpu.make_async_copy(entering.at[0, 0], first_in, entering_sem)
    front_copy = pltpu.make_async_copy(fronts_hbm, fronts, front_sem)
    green_copies = {
        start: pltpu.make_async_copy(
            green.at[0, 0, pl.ds(start, TILE)], operator.at[pl.ds(start, TILE)], green_sem.at[index]
        )
        for index, start in enumerate(tiles)
    }
    source_copies = [
        pltpu.make_async_copy(sources.at[tick, 0, 0], source_rows.at[tick], source_sem.at[tick])
        for tick in range(ticks)
    ]
    enter_copy.start()
    green_copies[tiles[0]].start()
    front_copy.start()
    source_copies[0].start()
    for start in tiles[1:]:
        green_copies[start].start()
    for tick in range(1, ticks):
        source_copies[tick].start()

    def live_factor(tick):
        front = gx + gy - tick
        met = jnp.int32(0)
        for b in range(fronts.shape[0]):
            met = met | (fronts[b] == front).astype(jnp.int32)
        return met.astype(jnp.float32)

    def place(h, low, high):
        return pl.ds(offsets[h] * blocks + low * CHUNKS[h], (high - low) * CHUNKS[h])

    zeros[...] = jnp.zeros(zeros.shape, jnp.bfloat16)
    for low, high, dx, dy in parts:
        @pl.when(jnp.logical_not(comes(dx, dy)))
        def _(low=low, high=high):
            for tick in range(ticks - 1):
                for h, size in enumerate(CHUNKS):
                    pltpu.make_async_copy(
                        zeros.at[pl.ds(0, (high - low) * size)], landed.at[tick, place(h, low, high)],
                        land_sem.at[tick, h],
                    ).start()

    def transfer(tick, h, index):
        low, high, _, _ = parts[index]
        return pltpu.make_async_remote_copy(
            src_ref=sent.at[tick, place(h, low, high)],
            dst_ref=landed.at[tick, place(h, low, high)],
            send_sem=send_sem.at[index],
            recv_sem=land_sem.at[tick, h],
            device_id=next_device[index],
            device_id_type=MESH,
        )

    def send(tick, h, index):
        ok = to_next[index]
        if index == 0:
            @pl.when(jnp.logical_and(ok, gx % 2 == 0))
            def _():
                transfer(tick, h, index).start()
        else:
            @pl.when(ok)
            def _():
                transfer(tick, h, index).start()
        if index == 1:
            @pl.when(jnp.logical_and(goes(0, 1), gx % 2 == 1))
            def _():
                transfer(tick, h, 0).start()

    def arrive(tick, h):
        whole = landed.at[tick, place(h, 0, blocks)]
        pltpu.make_async_copy(whole, whole, land_sem.at[tick, h]).wait()

    def send_ready(tick, h, done):
        for index, (low, high, _, _) in enumerate(parts):
            if index not in done[1] and all(b in done[0] for b in range(low, high)):
                send(tick, h, index)
                done[1].add(index)

    enter_copy.wait()
    rounded = first_in[...].astype(jnp.bfloat16)
    front_copy.wait()
    live = live_factor(0)
    source_copies[0].wait()
    done = (set(), set())
    waited = False
    for start in tiles:
        green_copies[start].wait()
        product = jnp.dot(operator[start:start + TILE, :], rounded, preferred_element_type=jnp.float32)
        if start < edge:
            product = product + source_rows[0, start:start + TILE, :].astype(jnp.float32)
        out = (product * live).astype(jnp.bfloat16).T
        for q in range(TILE // LANES):
            block = start // LANES + q
            for h, size in enumerate(CHUNKS):
                sent[0, place(h, block, block + 1)] = out[
                    offsets[h]:offsets[h] + size, q * LANES:(q + 1) * LANES
                ]
            done[0].add(block)
        if not waited and all(b in done[0] for b in range(parts[0][0], parts[0][1])):
            count = sum(goes(dx, dy).astype(jnp.int32) for _, _, dx, dy in parts)

            @pl.when(count > 0)
            def _():
                pl.semaphore_wait(barrier, count)
            waited = True
        if waited:
            send_ready(0, 0, done)
    for index in range(len(parts)):
        send(0, 1, index)
    for index in range(len(parts)):
        for h in range(2, len(CHUNKS)):
            send(0, h, index)

    for start in tiles:
        turned[:, start:start + TILE] = operator[start:start + TILE, :].T

    for tick in range(1, ticks):
        source_copies[tick].wait()
        if tick < ticks - 1:
            source_cols[tick] = source_rows[tick].T

    for tick in range(1, ticks - 1):
        live = live_factor(tick)
        for h, size in enumerate(CHUNKS):
            arrive(tick - 1, h)
            incoming = jnp.concatenate([landed[tick - 1, place(h, b, b + 1)] for b in range(blocks)], axis=1)
            done = (set(), set())
            for start in tiles:
                product = jnp.dot(incoming, turned[:, start:start + TILE], preferred_element_type=jnp.float32)
                if start < edge:
                    product = product + source_cols[
                        tick, offsets[h]:offsets[h] + size, start:start + TILE
                    ].astype(jnp.float32)
                out = (product * live).astype(jnp.bfloat16)
                for q in range(TILE // LANES):
                    block = start // LANES + q
                    sent[tick, place(h, block, block + 1)] = out[:, q * LANES:(q + 1) * LANES]
                    done[0].add(block)
                send_ready(tick, h, done)

    tick = ticks - 1
    live = live_factor(tick)
    for h, size in enumerate(CHUNKS):
        if h == final:
            for index, (low, high, dx, dy) in enumerate(parts):
                @pl.when(goes(dx, dy))
                def _(low=low, high=high, index=index):
                    whole = sent.at[:, pl.ds(0, (high - low) * width)]
                    pltpu.make_async_copy(whole, whole, send_sem.at[index]).wait()
        arrive(tick - 1, h)
        incoming = jnp.concatenate([landed[tick - 1, place(h, b, b + 1)] for b in range(blocks)], axis=1)
        for start in tiles:
            product = jnp.dot(incoming, turned[:, start:start + TILE], preferred_element_type=jnp.float32)
            if h < final:
                held_chunk[offsets[h]:offsets[h] + size, start:start + TILE] = product
            else:
                held = held_chunk[:, start:start + TILE]
                whole = jnp.concatenate([held, product], axis=0).T
                if start < edge:
                    whole = whole + source_rows[tick, start:start + TILE, :].astype(jnp.float32)
                last[0, 0, start:start + TILE, :] = whole * live


def local(green, sources, entering, start_front):
    ticks, edge = sources.shape[0], sources.shape[3]
    order, width = entering.shape[2], entering.shape[3]
    blocks = order // LANES
    n_tiles = order // TILE

    def body(*refs):
        sweep_kernel(ticks, order, edge // 2, width, *refs)

    hbm = pl.BlockSpec(memory_space=pltpu.HBM)
    return pl.pallas_call(
        body,
        name="sweep",
        out_shape=jax.ShapeDtypeStruct(entering.shape, jnp.float32),
        in_specs=[hbm, hbm, hbm, hbm],
        out_specs=pl.BlockSpec(memory_space=pltpu.VMEM),
        scratch_shapes=[
            pltpu.SMEM(start_front.shape, jnp.int32),
            pltpu.VMEM((order, order), jnp.bfloat16),
            pltpu.VMEM((order, order), jnp.bfloat16),
            pltpu.VMEM((ticks, edge, width), jnp.bfloat16),
            pltpu.VMEM((ticks, width, edge), jnp.bfloat16),
            pltpu.VMEM((order, width), jnp.float32),
            pltpu.VMEM((ticks - 1, blocks * width, LANES), jnp.bfloat16),
            pltpu.VMEM((ticks - 1, blocks * width, LANES), jnp.bfloat16),
            pltpu.VMEM((width - CHUNKS[-1], order), jnp.float32),
            pltpu.VMEM((edge // 2 // LANES * max(CHUNKS), LANES), jnp.bfloat16),
            pltpu.SemaphoreType.DMA,
            pltpu.SemaphoreType.DMA((n_tiles,)),
            pltpu.SemaphoreType.DMA((ticks,)),
            pltpu.SemaphoreType.DMA,
            pltpu.SemaphoreType.DMA((3,)),
            pltpu.SemaphoreType.DMA((ticks - 1, len(CHUNKS))),
        ],
        compiler_params=pltpu.CompilerParams(
            collective_id=0, has_side_effects=True, vmem_limit_bytes=32 * 1024 * 1024
        ),
        cost_estimate=pl.CostEstimate(
            flops=2 * ticks * order * order * width,
            bytes_accessed=2 * order * order + 2 * ticks * edge * width + 8 * order * width,
            transcendentals=0,
        ),
    )(*(pltpu.with_memory_space_constraint(a, pltpu.HBM) for a in (start_front, green, sources, entering)))


def solution(mesh):
    in_specs = (
        P("gx", "gy", None, None),
        P(None, "gx", "gy", None, None),
        P("gx", "gy", None, None),
        P(),
    )
    out_specs = P("gx", "gy", None, None)
    return jax.shard_map(local, mesh=mesh, in_specs=in_specs, out_specs=out_specs, check_vma=False)
```
